32 devices in a mesh: groups: 2 (over y), leaf: 4 (over z), rhs: 2 (over x), sub: 2 (over core).
Axes of the slice: x: 2, y: 2, z: 4, core: 2. Of those that a mesh axis runs over, the one named last changes fastest.
Arguments:
- densities: bfloat16 [64, 262144], P(None, ('groups', 'leaf', 'rhs', 'sub')), parts along dimension 1, may hold values from -6 to 6
- geometry: bfloat16 [4, 262144], P(None, ('groups', 'leaf', 'rhs', 'sub')), parts along dimension 1, may hold values from -0.31 to 1, as said below
- near_index: int32 [2048, 16], P(('groups', 'leaf', 'rhs', 'sub')), parts along dimension 0, may hold values from 0 to 1023, as said below
- leaf_basis: bfloat16 [2048, 32, 128], P(('groups', 'leaf', 'rhs', 'sub')), parts along dimension 0, may hold values from -0.5 to 0.5
- transfer_one: bfloat16 [512, 4, 32, 32], P(('groups', 'leaf', 'rhs', 'sub')), parts along dimension 0, may hold values from -0.75 to 0.75
- coupling_one: bfloat16 [512, 4, 32, 32], P(('groups', 'leaf', 'rhs', 'sub')), parts along dimension 0, may hold values from -0.375 to 0.375
- partners_one: int32 [512, 4], P(('groups', 'leaf', 'rhs', 'sub')), parts along dimension 0, may hold values from 0 to 255, as said below
- transfer_two: bfloat16 [128, 4, 32, 32], P(('groups', 'leaf', 'rhs', 'sub')), parts along dimension 0, may hold values from -0.75 to 0.75
- coupling_two: bfloat16 [128, 4, 32, 32], P(('groups', 'leaf', 'rhs', 'sub')), parts along dimension 0, may hold values from -0.25 to 0.25
- partners_two: int32 [128, 4], P(('groups', 'leaf', 'rhs', 'sub')), parts along dimension 0, may hold values from 0 to 63, as said below
- transfer_three: bfloat16 [32, 4, 32, 32], P(('groups', 'leaf', 'rhs', 'sub')), parts along dimension 0, may hold values from -0.75 to 0.75
- coupling_three: bfloat16 [32, 4, 32, 32], P(('groups', 'leaf', 'rhs', 'sub')), parts along dimension 0, may hold values from -0.1875 to 0.1875
- partners_three: int32 [32, 4], P(('groups', 'leaf', 'rhs', 'sub')), parts along dimension 0, may hold values from 0 to 15, as said below
- transfer_four: bfloat16 [8, 4, 32, 32], P('groups'), parts along dimension 0, may hold values from -0.75 to 0.75
- coupling_four: bfloat16 [8, 4, 32, 32], P('groups'), parts along dimension 0, may hold values from -0.125 to 0.125
- partners_four: int32 [8, 4], P('groups'), parts along dimension 0, may hold values from 0 to 3, as said below
Outputs:
- potential: bfloat16 [64, 262144], P(None, ('groups', 'leaf', 'rhs', 'sub')), parts along dimension 1
The draws below stay inside these ranges and needn't reach their ends.
There are 2 independent parts, one for each index of `groups`. The reference program is written for one: setup_inputs(seed, part) draws one part's arguments, and reference() takes and returns one part's arrays. A program takes and returns all parts, laid end to end along the dimension named above; each array names one. Nothing has to cross between parts.
Inputs may be any that keep to these rules, and one draw needn't show every extreme that they name: `geometry`: rows a and the quadrature weights w lie in [0, 1] and [0.002, 0.02], y and z lie in [-0.31, 0.31] with y^2 + z^2 close to 0.09. `near_index`: entry 0 of leaf i is i; the other entries of a row are distinct leaves (i + o) mod 1024 with 1 <= |o| <= 16; some leaf lists both o = -16 and o = 16. `partners_one`: entry k of node n is (n + o) mod 256 with 1 <= |o| <= 16; entries may repeat; some node lists both extremes. `partners_two`: entry k of node n is (n + o) mod 64 with 1 <= |o| <= 4; entries may repeat; some node lists both extremes. `partners_three`: entry k of node n is (n + o) mod 16 with |o| = 1; entries may repeat. `partners_four`: entry k of node n is (n + o) mod 4 with 1 <= |o| <= 2; entries may repeat.
All inputs are finite; a program needn't handle non-finite values.
Results may differ from the reference program's by a relative error of at most 0.0056.
Values may be sent and summed in bfloat16 or wider, within the bound.
A program may use at most 64 MiB of HBM per device.

```python
import math
import jax
import jax.numpy as jnp
from jax import lax

LEAF = 128
RANK = 32
RHS = 64
LPD = 64
NEAR = 16
REACH = 16
NCOUP = 4
LEAVES = 1024
POINTS = 131072
NODES1 = 256
NODES2 = 64
NODES3 = 16
NODES4 = 4


def draw_cycle_list(key, node_total, reach):
    magnitude_key, sign_key, chosen_key = jax.random.split(key, 3)
    magnitude = jax.random.randint(magnitude_key, (node_total, NCOUP), 1, reach + 1)
    sign_bits = jax.random.randint(sign_key, (node_total, NCOUP), 0, 2) * 2 - 1
    cycle_offset = magnitude * sign_bits
    chosen = jax.random.randint(chosen_key, (), 0, node_total)
    row_ids = jnp.arange(node_total, dtype=jnp.int32)[:, None]
    column_ids = jnp.arange(NCOUP, dtype=jnp.int32)[None, :]
    cycle_offset = jnp.where((row_ids == chosen) & (column_ids == 0), -reach, cycle_offset)
    cycle_offset = jnp.where((row_ids == chosen) & (column_ids == 1), reach, cycle_offset)
    return ((row_ids + cycle_offset) % node_total).astype(jnp.int32)


def draw_geometry(key, part):
    key = jax.random.fold_in(key, 3)
    axial_key, angle_key, weight_key = jax.random.split(key, 3)
    axial = jax.random.uniform(axial_key, (POINTS,), jnp.float32)
    angles = jax.random.uniform(angle_key, (POINTS,), jnp.float32, -math.pi, math.pi)
    weight = jnp.exp(jax.random.uniform(weight_key, (POINTS,), jnp.float32, math.log(0.002), math.log(0.02)))
    stacked = jnp.stack([axial, 0.3 * jnp.cos(angles), 0.3 * jnp.sin(angles), weight])
    return stacked.astype(jnp.bfloat16)


def draw_near_index(key, part):
    key = jax.random.fold_in(key, 5)
    score_key, chosen_key = jax.random.split(key, 2)
    width_total = 2 * REACH
    column_ids = jnp.arange(width_total, dtype=jnp.int32)
    candidates = jnp.where(column_ids < REACH, column_ids - REACH, column_ids - REACH + 1)
    scores = jax.random.randint(score_key, (LEAVES, width_total), 0, 2 ** 20) * width_total + column_ids[None, :]
    chosen = jax.random.randint(chosen_key, (), 0, LEAVES)
    row_ids = jnp.arange(LEAVES, dtype=jnp.int32)[:, None]
    forced = (row_ids == chosen) & ((column_ids[None, :] == 0) | (column_ids[None, :] == width_total - 1))
    scores = jnp.where(forced, scores + 2 ** 27, scores)
    top_slots = jax.lax.top_k(scores, NEAR - 1)[1]
    cycle_offset = jnp.concatenate([jnp.zeros((LEAVES, 1), jnp.int32), candidates[top_slots]], axis=1)
    return ((row_ids + cycle_offset) % LEAVES).astype(jnp.int32)


def draw_partners_one(key, part):
    key = jax.random.fold_in(key, 7)
    return draw_cycle_list(key, NODES1, LPD // 4)


def draw_partners_two(key, part):
    key = jax.random.fold_in(key, 11)
    return draw_cycle_list(key, NODES2, LPD // 16)


def draw_partners_three(key, part):
    key = jax.random.fold_in(key, 13)
    return draw_cycle_list(key, NODES3, 1)


def draw_partners_four(key, part):
    key = jax.random.fold_in(key, 17)
    return draw_cycle_list(key, NODES4, 2)


def block_levels(own_key, dims, cuts, smallest, high):
    level = 1.0
    for axis_at, parts in cuts:
        draws = jax.random.uniform(jax.random.fold_in(jax.random.fold_in(own_key, 6), axis_at), (parts,), jnp.float32, smallest / len(cuts), high / len(cuts))
        level = level * jnp.repeat(jnp.exp(draws), dims[axis_at] // parts).reshape((-1,) + (1,) * (len(dims) - 1 - axis_at))
    return level


def scatter_about(rng, shape, scale, bound, pieces=(), kind=jnp.bfloat16):
    gain = block_levels(rng, shape, pieces, -0.22, 0.18) if pieces else 1.0
    drawn = jax.random.normal(rng, shape, jnp.float32) * scale * gain
    return jnp.minimum(jnp.maximum(drawn, -bound), bound).astype(kind)


def setup_inputs(seed: int = 0, part: int = 0) -> dict:
    arg_keys = jax.random.split(jax.random.key(seed), 17)
    part_keys = jax.random.split(jax.random.fold_in(arg_keys[16], part), 17)
    densities = scatter_about(part_keys[0], (RHS, POINTS), 1.0, 6.0, ((1, 16),))
    geometry = draw_geometry(jax.random.fold_in(jax.random.fold_in(arg_keys[16], part), 71), part)
    near_index = draw_near_index(jax.random.fold_in(jax.random.fold_in(arg_keys[16], part), 71), part)
    leaf_basis = scatter_about(part_keys[3], (LEAVES, RANK, LEAF), LEAF ** -0.5, 0.5, ((0, 16),))
    transfer_one = scatter_about(part_keys[4], (NODES1, 4, RANK, RANK), (2 * RANK) ** -0.5, 0.75, ((0, 16),))
    coupling_one = scatter_about(part_keys[5], (NODES1, NCOUP, RANK, RANK), (NCOUP * RANK * 2) ** -0.5, 0.375, ((0, 16),))
    partners_one = draw_partners_one(jax.random.fold_in(jax.random.fold_in(arg_keys[16], part), 71), part)
    transfer_two = scatter_about(part_keys[7], (NODES2, 4, RANK, RANK), (2 * RANK) ** -0.5, 0.75, ((0, 16),))
    coupling_two = scatter_about(part_keys[8], (NODES2, NCOUP, RANK, RANK), (NCOUP * RANK * 4) ** -0.5, 0.25, ((0, 16),))
    partners_two = draw_partners_two(jax.random.fold_in(jax.random.fold_in(arg_keys[16], part), 71), part)
    transfer_three = scatter_about(part_keys[10], (NODES3, 4, RANK, RANK), (2 * RANK) ** -0.5, 0.75, ((0, 16),))
    coupling_three = scatter_about(part_keys[11], (NODES3, NCOUP, RANK, RANK), (NCOUP * RANK * 8) ** -0.5, 0.1875, ((0, 16),))
    partners_three = draw_partners_three(jax.random.fold_in(jax.random.fold_in(arg_keys[16], part), 71), part)
    transfer_four = scatter_about(part_keys[13], (NODES4, 4, RANK, RANK), (2 * RANK) ** -0.5, 0.75)
    coupling_four = scatter_about(part_keys[14], (NODES4, NCOUP, RANK, RANK), (NCOUP * RANK * 16) ** -0.5, 0.125)
    partners_four = draw_partners_four(jax.random.fold_in(jax.random.fold_in(arg_keys[16], part), 71), part)
    return {"densities": densities, "geometry": geometry, "near_index": near_index, "leaf_basis": leaf_basis, "transfer_one": transfer_one, "coupling_one": coupling_one, "partners_one": partners_one, "transfer_two": transfer_two, "coupling_two": coupling_two, "partners_two": partners_two, "transfer_three": transfer_three, "coupling_three": coupling_three, "partners_three": partners_three, "transfer_four": transfer_four, "coupling_four": coupling_four, "partners_four": partners_four}


spacing = 0.1
smoothing = 0.0025

def kernel_block(target_geometry, source_geometry, offset):
    target = target_geometry.astype(jnp.float32)
    source = source_geometry.astype(jnp.float32)
    axial = spacing * (offset.astype(jnp.float32)[:, :, None, None] + source[0][:, :, None, :] - target[0][:, None, :, None])
    across = source[1][:, :, None, :] - target[1][:, None, :, None]
    vertical = source[2][:, :, None, :] - target[2][:, None, :, None]
    distance = axial * axial + across * across + vertical * vertical + smoothing
    return (source[3][:, :, None, :] * lax.rsqrt(distance)).astype(jnp.bfloat16)

def lift_level(transfer, lower_coefs):
    node_total = transfer.shape[0]
    grouped = lower_coefs.reshape(node_total, 4, lower_coefs.shape[1], lower_coefs.shape[2])
    return jnp.einsum('nqab,nqbr->nar', transfer.astype(jnp.float32), grouped.astype(jnp.float32)).astype(jnp.bfloat16)

def couple_level(coupling, partners, coefficients):
    return jnp.einsum('nkab,nkbr->nar', coupling.astype(jnp.float32), coefficients[partners].astype(jnp.float32))

def lower_level(transfer, upper_grade):
    node_total = transfer.shape[0]
    spread = jnp.einsum('nqba,nbr->nqar', transfer.astype(jnp.float32), upper_grade.astype(jnp.float32))
    return spread.reshape(node_total * 4, upper_grade.shape[1], upper_grade.shape[2])

def reference(densities, geometry, near_index, leaf_basis, transfer_one, coupling_one, partners_one, transfer_two, coupling_two, partners_two, transfer_three, coupling_three, partners_three, transfer_four, coupling_four, partners_four):
    leaf_total = near_index.shape[0]
    rhs_size = densities.shape[0]
    leaf_size = leaf_basis.shape[2]
    dens_leaves = densities.reshape(rhs_size, leaf_total, leaf_size)
    geometry_leaves = geometry.reshape(4, leaf_total, leaf_size)
    block_rows = 64
    block_steps = leaf_total // block_rows

    def one_block(first_leaf):
        source_slots = lax.dynamic_slice_in_dim(near_index, first_leaf, block_rows, 0)
        leaf_ids = first_leaf + jnp.arange(block_rows, dtype=jnp.int32)
        cycle_offset = (source_slots - leaf_ids[:, None] + leaf_total // 2) % leaf_total - leaf_total // 2
        target = lax.dynamic_slice_in_dim(geometry_leaves, first_leaf, block_rows, 1)
        kernel_vals = kernel_block(target, geometry_leaves[:, source_slots], cycle_offset)
        source_dens = dens_leaves[:, source_slots]
        return jnp.einsum('rbks,bkts->rbt', source_dens.astype(jnp.float32), kernel_vals.astype(jnp.float32))
    block_starts = jnp.arange(block_steps, dtype=jnp.int32) * block_rows
    block_terms = lax.map(one_block, block_starts)
    near_field = jnp.moveaxis(block_terms, 0, 1).reshape(rhs_size, leaf_total, leaf_size)
    coef_zero = jnp.einsum('nap,rnp->nar', leaf_basis.astype(jnp.float32), dens_leaves.astype(jnp.float32)).astype(jnp.bfloat16)
    coef_one = lift_level(transfer_one, coef_zero)
    coef_two = lift_level(transfer_two, coef_one)
    coef_three = lift_level(transfer_three, coef_two)
    coef_four = lift_level(transfer_four, coef_three)
    field_one = couple_level(coupling_one, partners_one, coef_one)
    field_two = couple_level(coupling_two, partners_two, coef_two)
    field_three = couple_level(coupling_three, partners_three, coef_three)
    field_four = couple_level(coupling_four, partners_four, coef_four)
    grade_four = field_four.astype(jnp.bfloat16)
    grade_three = (field_three + lower_level(transfer_four, grade_four)).astype(jnp.bfloat16)
    grade_two = (field_two + lower_level(transfer_three, grade_three)).astype(jnp.bfloat16)
    grade_one = (field_one + lower_level(transfer_two, grade_two)).astype(jnp.bfloat16)
    grade_zero = lower_level(transfer_one, grade_one).astype(jnp.bfloat16)
    far_field = jnp.einsum('nar,nap->rnp', grade_zero.astype(jnp.float32), leaf_basis.astype(jnp.float32))
    return (near_field + far_field).astype(jnp.bfloat16).reshape(rhs_size, leaf_total * leaf_size)
```

```python
import functools

import jax
import jax.numpy as jnp
from jax import lax
from jax.experimental import pallas as pl
from jax.experimental.pallas import tpu as pltpu
from jax.sharding import PartitionSpec as P

AXES = ("leaf", "rhs", "sub")
REACH = 16
SPACING2 = 0.01
SMOOTH = 0.0025
f32 = jnp.float32
bf16 = jnp.bfloat16


def dot(a, b, ca, cb):
    return lax.dot_general(a, b, (((ca,), (cb,)), ((), ())), preferred_element_type=f32)


def wrap(d, total):
    d = jnp.where(d >= total // 2, d - total, d)
    return jnp.where(d < -(total // 2), d + total, d)


def split3(v):
    hi = v.astype(bf16).astype(f32)
    r1 = v - hi
    mid = r1.astype(bf16).astype(f32)
    return r1, r1 - mid


def up_kernel(dens, basis, t1, t2, t3, out, c0):
    leaves = basis.shape[0]
    rank = basis.shape[1]
    n1, n2, n3 = t1.shape[0], t2.shape[0], t3.shape[0]
    for i in range(leaves):
        c0[i] = dot(basis[i], dens[:, i * 128 : (i + 1) * 128], 1, 1).astype(bf16)

    def lift(t, count, source, base, into):
        for n in range(count):
            acc = dot(t[n, 0], source[base + 4 * n], 1, 0)
            for q in range(1, 4):
                acc += dot(t[n, q], source[base + 4 * n + q], 1, 0)
            out[into + n] = acc.astype(bf16)

    lift(t1, n1, c0, 0, 0)
    lift(t2, n2, out, 0, n1)
    lift(t3, n3, out, n1, n1 + n2)


def near_kernel(shards, near_index, dens, geom, left, right, out, densw, fa, fb, tf):
    leaves = near_index.shape[0]
    near = near_index.shape[1]
    rhs = dens.shape[0]
    total = leaves * shards
    me = lax.axis_index(AXES)
    row8 = lax.broadcasted_iota(jnp.int32, (8, 128), 0)
    first = (row8 == 0) | (row8 == 3) | (row8 >= 6)
    second = (row8 == 1) | (row8 == 4)

    def prepare(slot, d, g, own):
        g = g.astype(f32)
        a, y, z, w = (g[r : r + 1] for r in range(4))
        densw[slot] = (d.astype(f32) * w).astype(bf16)
        a8, y8, z8 = (jnp.broadcast_to(v, (8, 128)) for v in (a, y, z))
        square = SPACING2 * a8 * a8 + y8 * y8 + z8 * z8
        fa[slot] = jnp.where(
            row8 < 3, square + SMOOTH,
            jnp.where(row8 < 6, (-2.0 * SPACING2) * a8, jnp.where(row8 == 6, -2.0 * y8, -2.0 * z8)),
        )
        fb[slot] = jnp.where(row8 < 3, (2.0 * SPACING2) * a8, jnp.where(row8 < 6, -2.0 * SPACING2, 0.0))
        if own:
            r1, r2 = split3(square)
            upper = jnp.where(row8 < 3, 1.0, jnp.where(row8 < 6, a8, jnp.where(row8 == 6, y8, z8)))
            lower = jnp.where(row8 == 0, square, jnp.where(row8 == 1, r1, jnp.where(row8 == 2, r2, 0.0)))
            tf[slot - REACH] = jnp.concatenate([upper, lower], axis=0).astype(bf16)

    for j in range(REACH):
        cols = slice(j * 128, (j + 1) * 128)
        prepare(j, left[:rhs, cols], left[rhs:, cols], False)
        prepare(REACH + leaves + j, right[:rhs, cols], right[rhs:, cols], False)
    for j in range(leaves):
        cols = slice(j * 128, (j + 1) * 128)
        prepare(REACH + j, dens[:, cols], geom[:, cols], True)

    quad = jnp.where(row8 < 3, SPACING2, 0.0)
    tail = jnp.where(row8 < 3, 1.0, 0.0)

    def source(i, k):
        o = wrap(near_index[i, k] - (me * leaves + i), total)
        pos = i + REACH + o
        of = o.astype(f32)
        v = fa[pos] + of * (fb[pos] + of * quad)
        r1, r2 = split3(v)
        x = jnp.where(first, v, jnp.where(second, r1, r2))
        return jnp.concatenate([x, tail], axis=0).astype(bf16), densw[pos]

    def one(i, carry):
        target = tf[i]
        acc = None
        for k in range(0, near, 2):
            x0, d0 = source(i, k)
            x1, d1 = source(i, k + 1)
            dist = dot(target, jnp.concatenate([x0, x1], axis=1), 0, 0)
            block = lax.rsqrt(dist.astype(bf16))
            term = dot(block, jnp.concatenate([d0, d1], axis=1), 1, 1)
            acc = term if acc is None else acc + term
        out[:, pl.ds(pl.multiple_of(i * 128, 128), 128)] = acc.T
        return carry

    lax.fori_loop(0, leaves, one, 0)


def down_kernel(
    shards, p1, p2, p3, p4, own, left, right, three, c1, c2, c3, c4, t1, t2, t3, t4, basis, nearf, out, wide
):
    n1, n2 = c1.shape[0], c2.shape[0]
    me = lax.axis_index(AXES)
    leaves = basis.shape[0]
    spans = ((0, n1), (n1, n2), (n1 + n2, 1))
    bases = (0, 3 * n1, 3 * (n1 + n2))
    for (lo, n), base in zip(spans, bases):
        for m in range(n):
            wide[base + m] = left[lo + m]
            wide[base + n + m] = own[lo + m]
            wide[base + 2 * n + m] = right[lo + m]

    def couple(c, p, level, n):
        count = spans[level][1]
        acc = None
        for k in range(4):
            o = wrap(p[n, k] - (me * count + n), count * shards)
            term = dot(c[n, k], wide[bases[level] + count + n + o], 1, 0)
            acc = term if acc is None else acc + term
        return acc

    node = me // 4
    field4 = None
    for k in range(4):
        q4 = p4[node, k]
        acc = None
        for q in range(4):
            term = dot(t4[q4, q], three[4 * q4 + q], 1, 0)
            acc = term if acc is None else acc + term
        term = dot(c4[node, k], acc.astype(bf16), 1, 0)
        field4 = term if field4 is None else field4 + term
    g4 = field4.astype(bf16)
    g3 = (couple(c3, p3, 2, 0) + dot(t4[node, me % 4], g4, 0, 0)).astype(bf16)
    for m in range(n2):
        g2 = (couple(c2, p2, 1, m) + dot(t3[0, m], g3, 0, 0)).astype(bf16)
        for q in range(4):
            n = 4 * m + q
            g1 = (couple(c1, p1, 0, n) + dot(t2[m, q], g2, 0, 0)).astype(bf16)
            for r in range(4):
                i = 4 * n + r
                g0 = dot(t1[n, r], g1, 0, 0).astype(bf16)
                far = dot(g0, basis[i], 0, 0)
                cols = slice(i * 128, (i + 1) * 128)
                out[:, cols] = (nearf[:, cols] + far).astype(bf16)


VM = pl.BlockSpec(memory_space=pltpu.VMEM)
SM = pl.BlockSpec(memory_space=pltpu.SMEM)


def shift(v, step):
    count = lax.axis_size(AXES)
    return lax.ppermute(v, AXES, [(i, (i + step) % count) for i in range(count)])


def body(
    densities, geometry, near_index, leaf_basis,
    transfer_one, coupling_one, partners_one,
    transfer_two, coupling_two, partners_two,
    transfer_three, coupling_three, partners_three,
    transfer_four, coupling_four, partners_four,
):
    shards = lax.axis_size(AXES)
    leaves, rank, _ = leaf_basis.shape
    rhs, points = densities.shape
    n1, n2 = transfer_one.shape[0], transfer_two.shape[0]
    nodes = n1 + n2 + 1
    params = pltpu.CompilerParams(vmem_limit_bytes=40 * 2**20)
    width = REACH * 128
    tail = jnp.concatenate([densities[:, points - width :], geometry[:, points - width :]], axis=0)
    head = jnp.concatenate([densities[:, :width], geometry[:, :width]], axis=0)
    left = shift(tail, 1)
    right = shift(head, -1)

    coefs = pl.pallas_call(
        up_kernel,
        out_shape=jax.ShapeDtypeStruct((nodes, rank, rhs), bf16),
        in_specs=[VM] * 5,
        out_specs=VM,
        scratch_shapes=[pltpu.VMEM((leaves, rank, rhs), bf16)],
        compiler_params=params,
        name="up",
        cost_estimate=pl.CostEstimate(flops=10**8, bytes_accessed=2 * 10**6, transcendentals=0),
    )(densities, leaf_basis, transfer_one, transfer_two, transfer_three)
    cleft = shift(coefs, 1)
    cright = shift(coefs, -1)
    three = lax.all_gather(coefs[nodes - 1].reshape(1, -1), AXES, axis=0, tiled=True)
    three = three.reshape(shards, rank, rhs)

    wide = leaves + 2 * REACH
    nearf = pl.pallas_call(
        functools.partial(near_kernel, shards),
        out_shape=jax.ShapeDtypeStruct((rhs, points), f32),
        in_specs=[SM] + [VM] * 4,
        out_specs=VM,
        scratch_shapes=[
            pltpu.VMEM((wide, rhs, 128), bf16),
            pltpu.VMEM((wide, 8, 128), f32),
            pltpu.VMEM((wide, 8, 128), f32),
            pltpu.VMEM((leaves, 16, 128), bf16),
        ],
        compiler_params=params,
        name="near",
        cost_estimate=pl.CostEstimate(flops=2 * 10**10, bytes_accessed=5 * 10**6, transcendentals=16 * 10**6),
    )(near_index, densities, geometry, left, right)

    return pl.pallas_call(
        functools.partial(down_kernel, shards),
        out_shape=jax.ShapeDtypeStruct((rhs, points), bf16),
        in_specs=[SM] * 4 + [VM] * 14,
        out_specs=VM,
        scratch_shapes=[pltpu.VMEM((3 * nodes, rank, rhs), bf16)],
        compiler_params=params,
        name="down",
        cost_estimate=pl.CostEstimate(flops=10**8, bytes_accessed=5 * 10**6, transcendentals=0),
    )(
        partners_one, partners_two, partners_three, partners_four,
        coefs, cleft, cright, three,
        coupling_one, coupling_two, coupling_three, coupling_four,
        transfer_one, transfer_two, transfer_three, transfer_four,
        leaf_basis, nearf,
    )


def solution(mesh):
    every = ("groups", "leaf", "rhs", "sub")
    split = lambda n: P(every, *([None] * n))
    level = [split(3), split(3), split(1)]
    in_specs = (
        P(None, every), P(None, every), split(1), split(2),
        *level, *level, *level,
        P("groups", None, None, None), P("groups", None, None, None), P("groups", None),
    )
    return jax.shard_map(body, mesh=mesh, in_specs=in_specs, out_specs=P(None, every), check_vma=False)
```

```python
import functools

import jax
import jax.numpy as jnp
from jax import lax
from jax.experimental import pallas as pl
from jax.experimental.pallas import tpu as pltpu
from jax.sharding import PartitionSpec as P

AXES = ("leaf", "rhs", "sub")
REACH = 16
FAR = 11
SPACING2 = 0.01
SMOOTH = 0.0025
GROUP = 2
FLIP = False
UNROLL = 8
f32 = jnp.float32
bf16 = jnp.bfloat16


def dot(a, b, ca, cb):
    return lax.dot_general(a, b, (((ca,), (cb,)), ((), ())), preferred_element_type=f32)


def wrap(d, total):
    d = jnp.where(d >= total // 2, d - total, d)
    return jnp.where(d < -(total // 2), d + total, d)


def split3(v):
    hi = v.astype(bf16).astype(f32)
    r1 = v - hi
    mid = r1.astype(bf16).astype(f32)
    return r1, r1 - mid


def peers(shards):
    if shards <= 2 * FAR + 1:
        return list(range(1, shards)), shards
    return [d for d in range(-FAR, FAR + 1) if d], 2 * FAR + 1


def slot_of(d, shards):
    if shards <= 2 * FAR + 1:
        return d % shards
    return d + FAR


def exchange_kernel(
    shards, rhs_axis, sub_axis,
    dens, geom, basis, t1, t2, t3,
    own, cleft, cright, three, dleft, dright, gleft, gright,
    c0, stage, send, recv,
):
    leaves = basis.shape[0]
    n1, n2 = t1.shape[0], t2.shape[0]
    nodes = own.shape[0]
    width = dleft.shape[1]
    points = dens.shape[1]
    me = lax.axis_index(AXES)
    offsets, _ = peers(shards)

    def at(step):
        s = lax.rem(me + step + shards, shards)
        return {
            "leaf": s // (rhs_axis * sub_axis),
            "rhs": (s // sub_axis) % rhs_axis,
            "sub": s % sub_axis,
        }

    def copy(src, dst, index, step):
        return pltpu.make_async_remote_copy(
            src_ref=src, dst_ref=dst, send_sem=send.at[index], recv_sem=recv.at[index],
            device_id=at(step), device_id_type=pl.DeviceIdType.MESH,
        )

    barrier = pltpu.get_barrier_semaphore()
    for d in offsets:
        pl.semaphore_signal(barrier, inc=1, device_id=at(d), device_id_type=pl.DeviceIdType.MESH)
    stage[...] = jnp.zeros_like(stage)
    stage[0, 0:4] = geom[:, points - width :]
    stage[1, 0:4] = geom[:, :width]
    pl.semaphore_wait(barrier, len(offsets))

    copies = [
        copy(dens.at[:, pl.ds(points - width, width)], dleft, 0, 1),
        copy(dens.at[:, pl.ds(0, width)], dright, 1, -1),
        copy(stage.at[0], gleft, 2, 1),
        copy(stage.at[1], gright, 3, -1),
    ]
    for c in copies:
        c.start()

    def leaf_coefs(g, carry):
        for u in range(16):
            i = g * 16 + u
            cols = pl.ds(pl.multiple_of(i * 128, 128), 128)
            c0[i] = dot(dens[:, cols], basis[i], 1, 1).astype(bf16)
        return carry

    lax.fori_loop(0, leaves // 16, leaf_coefs, 0)

    def lift(t, n, source, base, into):
        acc = None
        for q in range(4):
            term = dot(source[base + 4 * n + q], t[n, q], 1, 1)
            acc = term if acc is None else acc + term
        own[into + n] = acc.astype(bf16)

    for n in range(n1):
        lift(t1, n, c0, 0, 0)
    for n in range(n2):
        lift(t2, n, own, 0, n1)
    lift(t3, 0, own, n1, n1 + n2)

    more = [copy(own.at[nodes - 1], three.at[slot_of(-d, shards)], 6 + x, d) for x, d in enumerate(offsets)]
    more += [copy(own, cleft, 4, 1), copy(own, cright, 5, -1)]
    for c in more:
        c.start()
    three[slot_of(0, shards)] = own[nodes - 1]
    for c in more + copies:
        c.wait()


def main_kernel(
    shards, near_index, p1, p2, p3, p4,
    dens, geom, dleft, dright, gleft, gright,
    own, cleft, cright, three,
    c1, c2, c3, c4, t1, t2, t3, t4, basis,
    out, wide, densw, fa, fb, tf, grade,
):
    leaves = near_index.shape[0]
    near = near_index.shape[1]
    total = leaves * shards
    me = lax.axis_index(AXES)
    n1, n2 = c1.shape[0], c2.shape[0]

    spans = ((0, n1), (n1, n2), (n1 + n2, 1))
    bases = (0, 3 * n1, 3 * (n1 + n2))
    for (lo, n), base in zip(spans, bases):
        for m in range(n):
            wide[base + m] = cleft[lo + m]
            wide[base + n + m] = own[lo + m]
            wide[base + 2 * n + m] = cright[lo + m]

    def couple(c, p, level, n):
        count = spans[level][1]
        acc = None
        for k in range(4):
            o = wrap(p[n, k] - (me * count + n), count * shards)
            term = dot(wide[bases[level] + count + n + o], c[n, k], 1, 1)
            acc = term if acc is None else acc + term
        return acc

    node = me // 4
    field4 = None
    for k in range(4):
        q4 = p4[node, k]
        acc = None
        for q in range(4):
            d = wrap(4 * q4 + q - me, shards)
            slot = jnp.where(d < 0, d + shards, d) if shards <= 2 * FAR + 1 else d + FAR
            term = dot(three[slot], t4[q4, q], 1, 1)
            acc = term if acc is None else acc + term
        term = dot(acc.astype(bf16), c4[node, k], 1, 1)
        field4 = term if field4 is None else field4 + term
    g4 = field4.astype(bf16)
    g3 = (couple(c3, p3, 2, 0) + dot(g4, t4[node, me % 4], 1, 0)).astype(bf16)
    f2 = [couple(c2, p2, 1, m) for m in range(n2)]
    f1 = [couple(c1, p1, 0, n) for n in range(n1)]
    g2 = [(f2[m] + dot(g3, t3[0, m], 1, 0)).astype(bf16) for m in range(n2)]
    for n in range(n1):
        grade[n] = (f1[n] + dot(g2[n // 4], t2[n // 4, n % 4], 1, 0)).astype(bf16)

    row8 = lax.broadcasted_iota(jnp.int32, (8, 128), 0)
    first = (row8 == 0) | (row8 == 3) | (row8 >= 6)
    second = (row8 == 1) | (row8 == 4)

    def prepare(slot, d, g, mine):
        g = g.astype(f32)
        a, y, z, w = (g[r : r + 1] for r in range(4))
        densw[slot] = (d.astype(f32) * w).astype(bf16)
        a8, y8, z8 = (jnp.broadcast_to(v, (8, 128)) for v in (a, y, z))
        square = SPACING2 * a8 * a8 + y8 * y8 + z8 * z8
        fa[slot] = jnp.where(
            row8 < 3, square + SMOOTH,
            jnp.where(row8 < 6, (-2.0 * SPACING2) * a8, jnp.where(row8 == 6, -2.0 * y8, -2.0 * z8)),
        )
        fb[slot] = jnp.where(row8 < 3, (2.0 * SPACING2) * a8, jnp.where(row8 < 6, -2.0 * SPACING2, 0.0))
        if mine:
            r1, r2 = split3(square)
            upper = jnp.where(row8 < 3, 1.0, jnp.where(row8 < 6, a8, jnp.where(row8 == 6, y8, z8)))
            lower = jnp.where(row8 == 0, square, jnp.where(row8 == 1, r1, jnp.where(row8 == 2, r2, 0.0)))
            tf[slot - REACH] = jnp.concatenate([upper, lower], axis=0).T.astype(bf16)

    for j in range(REACH):
        cols = slice(j * 128, (j + 1) * 128)
        prepare(j, dleft[:, cols], gleft[:, cols], False)
        prepare(REACH + leaves + j, dright[:, cols], gright[:, cols], False)
    for j in range(leaves):
        cols = slice(j * 128, (j + 1) * 128)
        prepare(REACH + j, dens[:, cols], geom[:, cols], True)

    quad = jnp.where(row8 < 3, SPACING2, 0.0)
    tail = jnp.where(row8 < 3, 1.0, 0.0)

    def source(i, k):
        o = wrap(near_index[i, k] - (me * leaves + i), total)
        pos = i + REACH + o
        of = o.astype(f32)
        v = fa[pos] + of * (fb[pos] + of * quad)
        r1, r2 = split3(v)
        x = jnp.where(first, v, jnp.where(second, r1, r2))
        return jnp.concatenate([x, tail], axis=0).astype(bf16), densw[pos]

    def one(i, carry):
        target = tf[i]
        node1 = i // 4
        g0 = dot(grade[node1], t1[node1, i % 4], 1, 0).astype(bf16)
        far = dot(g0, basis[i], 1, 0)
        acc = None
        for k in range(0, near, GROUP):
            xs, ds = zip(*[source(i, k + u) for u in range(GROUP)])
            dist = dot(target, jnp.concatenate(xs, axis=1), 1, 0)
            block = lax.rsqrt(dist.astype(bf16))
            d = jnp.concatenate(ds, axis=1)
            term = dot(d, block, 1, 1) if FLIP else dot(block, d, 1, 1)
            acc = term if acc is None else acc + term
        nearf = acc if FLIP else acc.T
        out[:, pl.ds(pl.multiple_of(i * 128, 128), 128)] = (nearf + far).astype(bf16)
        return carry

    lax.fori_loop(0, leaves, one, 0, unroll=UNROLL)


VM = pl.BlockSpec(memory_space=pltpu.VMEM)
SM = pl.BlockSpec(memory_space=pltpu.SMEM)


def body(
    densities, geometry, near_index, leaf_basis,
    transfer_one, coupling_one, partners_one,
    transfer_two, coupling_two, partners_two,
    transfer_three, coupling_three, partners_three,
    transfer_four, coupling_four, partners_four,
):
    shards = lax.axis_size(AXES)
    leaves, rank, _ = leaf_basis.shape
    rhs, points = densities.shape
    n1, n2 = transfer_one.shape[0], transfer_two.shape[0]
    nodes = n1 + n2 + 1
    width = REACH * 128
    offsets, slots = peers(shards)
    coef = jax.ShapeDtypeStruct((nodes, rhs, rank), bf16)
    side = jax.ShapeDtypeStruct((rhs, width), bf16)
    sideg = jax.ShapeDtypeStruct((16, width), bf16)

    own, cleft, cright, three, dleft, dright, gleft, gright = pl.pallas_call(
        functools.partial(exchange_kernel, shards, lax.axis_size("rhs"), lax.axis_size("sub")),
        out_shape=(
            coef, coef, coef, jax.ShapeDtypeStruct((slots, rhs, rank), bf16),
            side, side, sideg, sideg,
        ),
        in_specs=[VM] * 6,
        out_specs=(VM,) * 8,
        scratch_shapes=[
            pltpu.VMEM((leaves, rhs, rank), bf16),
            pltpu.VMEM((2, 16, width), bf16),
            pltpu.SemaphoreType.DMA((6 + len(offsets),)),
            pltpu.SemaphoreType.DMA((6 + len(offsets),)),
        ],
        compiler_params=pltpu.CompilerParams(
            vmem_limit_bytes=40 * 2**20, collective_id=0, has_side_effects=True
        ),
        name="exchange",
    )(densities, geometry, leaf_basis, transfer_one, transfer_two, transfer_three)

    wide = leaves + 2 * REACH
    return pl.pallas_call(
        functools.partial(main_kernel, shards),
        out_shape=jax.ShapeDtypeStruct((rhs, points), bf16),
        in_specs=[SM] * 5 + [VM] * 19,
        out_specs=VM,
        scratch_shapes=[
            pltpu.VMEM((3 * nodes, rhs, rank), bf16),
            pltpu.VMEM((wide, rhs, 128), bf16),
            pltpu.VMEM((wide, 8, 128), f32),
            pltpu.VMEM((wide, 8, 128), f32),
            pltpu.VMEM((leaves, 128, 16), bf16),
            pltpu.VMEM((n1, rhs, rank), bf16),
        ],
        compiler_params=pltpu.CompilerParams(vmem_limit_bytes=48 * 2**20),
        name="main",
    )(
        near_index, partners_one, partners_two, partners_three, partners_four,
        densities, geometry, dleft, dright, gleft, gright,
        own, cleft, cright, three,
        coupling_one, coupling_two, coupling_three, coupling_four,
        transfer_one, transfer_two, transfer_three, transfer_four,
        leaf_basis,
    )


def solution(mesh):
    every = ("groups", "leaf", "rhs", "sub")
    split = lambda n: P(every, *([None] * n))
    level = [split(3), split(3), split(1)]
    in_specs = (
        P(None, every), P(None, every), split(1), split(2),
        *level, *level, *level,
        P("groups", None, None, None), P("groups", None, None, None), P("groups", None),
    )
    return jax.shard_map(body, mesh=mesh, in_specs=in_specs, out_specs=P(None, every), check_vma=False)
```

```python
import functools

import jax
import jax.numpy as jnp
from jax import lax
from jax.experimental import pallas as pl
from jax.experimental.pallas import tpu as pltpu
from jax.sharding import PartitionSpec as P

AXES = ("leaf", "rhs", "sub")
REACH = 16
FAR = 11
SPACING2 = 0.01
SMOOTH = 0.0025
GROUP = 2
UNROLL = 8
f32 = jnp.float32
bf16 = jnp.bfloat16


def dot(a, b, ca, cb):
    return lax.dot_general(a, b, (((ca,), (cb,)), ((), ())), preferred_element_type=f32)


def wrap(d, total):
    d = jnp.where(d >= total // 2, d - total, d)
    return jnp.where(d < -(total // 2), d + total, d)


def split3(v):
    hi = v.astype(bf16).astype(f32)
    r1 = v - hi
    mid = r1.astype(bf16).astype(f32)
    return r1, r1 - mid


def peers(shards):
    if shards <= 2 * FAR + 1:
        return list(range(1, shards)), shards
    return [d for d in range(-FAR, FAR + 1) if d], 2 * FAR + 1


def slot_of(d, shards):
    if shards <= 2 * FAR + 1:
        return d % shards
    return d + FAR


def whole_kernel(
    shards, rhs_axis, sub_axis,
    near_index, p1, p2, p3, p4,
    dens_hbm, geom_hbm, basis_hbm, t1_hbm, t2_hbm, t3_hbm, t4_hbm, c1_hbm, c2_hbm, c3_hbm, c4_hbm,
    out,
    dens, geom, basis, t1, t2, t3, t4, c1, c2, c3, c4,
    own, cleft, cright, three, dleft, dright, gleft, gright,
    c0, stage, wide, densw, fa, fb, tf, grade, nearf,
    load, send, recv,
):
    leaves = basis.shape[0]
    near = near_index.shape[0]
    total = leaves * shards
    n1, n2 = t1.shape[0], t2.shape[0]
    nodes = own.shape[0]
    width = dleft.shape[1]
    points = dens.shape[1]
    me = lax.axis_index(AXES)
    offsets, _ = peers(shards)

    pairs = (
        (dens_hbm, dens), (geom_hbm, geom), (basis_hbm, basis), (t1_hbm, t1), (t2_hbm, t2), (t3_hbm, t3),
        (t4_hbm, t4), (c1_hbm, c1), (c2_hbm, c2), (c3_hbm, c3), (c4_hbm, c4),
    )
    loads = [pltpu.make_async_copy(src, dst, load.at[x]) for x, (src, dst) in enumerate(pairs)]
    for c in loads:
        c.start()

    def at(step):
        s = lax.rem(me + step + shards, shards)
        return {
            "leaf": s // (rhs_axis * sub_axis),
            "rhs": (s // sub_axis) % rhs_axis,
            "sub": s % sub_axis,
        }

    def copy(src, dst, index, step):
        return pltpu.make_async_remote_copy(
            src_ref=src, dst_ref=dst, send_sem=send.at[index], recv_sem=recv.at[index],
            device_id=at(step), device_id_type=pl.DeviceIdType.MESH,
        )

    barrier = pltpu.get_barrier_semaphore()
    for d in offsets:
        pl.semaphore_signal(barrier, inc=1, device_id=at(d), device_id_type=pl.DeviceIdType.MESH)
    stage[...] = jnp.zeros_like(stage)
    loads[0].wait()
    loads[1].wait()
    stage[0, 0:4] = geom[:, points - width :]
    stage[1, 0:4] = geom[:, :width]
    loads[2].wait()

    def leaf_coefs(g, carry):
        for u in range(16):
            i = g * 16 + u
            cols = pl.ds(pl.multiple_of(i * 128, 128), 128)
            c0[i] = dot(dens[:, cols], basis[i], 1, 1).astype(bf16)
        return carry

    lax.fori_loop(0, leaves // 16, leaf_coefs, 0)
    for c in loads[3:6]:
        c.wait()

    def lift(t, n, source, base, into):
        acc = None
        for q in range(4):
            term = dot(source[base + 4 * n + q], t[n, q], 1, 1)
            acc = term if acc is None else acc + term
        own[into + n] = acc.astype(bf16)

    for n in range(n1):
        lift(t1, n, c0, 0, 0)
    for n in range(n2):
        lift(t2, n, own, 0, n1)
    lift(t3, 0, own, n1, n1 + n2)
    pl.semaphore_wait(barrier, len(offsets))

    halos = [
        copy(dens.at[:, pl.ds(points - width, width)], dleft, 0, 1),
        copy(dens.at[:, pl.ds(0, width)], dright, 1, -1),
        copy(stage.at[0], gleft, 2, 1),
        copy(stage.at[1], gright, 3, -1),
    ]
    more = [copy(own.at[nodes - 1], three.at[slot_of(-d, shards)], 6 + x, d) for x, d in enumerate(offsets)]
    more += [copy(own, cleft, 4, 1), copy(own, cright, 5, -1)]
    for c in halos + more:
        c.start()
    three[slot_of(0, shards)] = own[nodes - 1]

    row8 = lax.broadcasted_iota(jnp.int32, (8, 128), 0)
    first = (row8 == 0) | (row8 == 3) | (row8 >= 6)
    second = (row8 == 1) | (row8 == 4)

    def prepare(slot, d, gb, mine):
        densw[slot] = d * gb[3:4]
        g = gb.astype(f32)
        a8, y8, z8 = (jnp.broadcast_to(g[r : r + 1], (8, 128)) for r in range(3))
        square = SPACING2 * a8 * a8 + y8 * y8 + z8 * z8
        fa[slot] = jnp.where(
            row8 < 3, square + SMOOTH,
            jnp.where(row8 < 6, (-2.0 * SPACING2) * a8, jnp.where(row8 == 6, -2.0 * y8, -2.0 * z8)),
        )
        fb[slot] = jnp.where(row8 < 3, (2.0 * SPACING2) * a8, jnp.where(row8 < 6, -2.0 * SPACING2, 0.0))
        if mine:
            r1, r2 = split3(square)
            upper = jnp.where(row8 < 3, 1.0, jnp.where(row8 < 6, a8, jnp.where(row8 == 6, y8, z8)))
            lower = jnp.where(row8 == 0, square, jnp.where(row8 == 1, r1, jnp.where(row8 == 2, r2, 0.0)))
            tf[slot - REACH] = jnp.concatenate([upper, lower], axis=0).T.astype(bf16)

    def prepare_own(g, carry):
        for u in range(16):
            j = g * 16 + u
            cols = pl.ds(pl.multiple_of(j * 128, 128), 128)
            prepare(REACH + j, dens[:, cols], geom[:, cols], True)
        return carry

    lax.fori_loop(0, leaves // 16, prepare_own, 0)

    quad = jnp.where(row8 < 3, SPACING2, 0.0)
    tail = jnp.where(row8 < 3, 1.0, 0.0)

    def source(i, k):
        o = wrap(near_index[k, i] - (me * leaves + i), total)
        pos = jnp.clip(i + REACH + o, 0, leaves + 2 * REACH - 1)
        of = o.astype(f32)
        v = fa[pos] + of * (fb[pos] + of * quad)
        r1, r2 = split3(v)
        x = jnp.where(first, v, jnp.where(second, r1, r2))
        return jnp.concatenate([x, tail], axis=0).astype(bf16), densw[pos]

    def near_leaf(i):
        target = tf[i]
        acc = None
        for k in range(0, near, GROUP):
            xs, ds = zip(*[source(i, k + u) for u in range(GROUP)])
            dist = dot(target, jnp.concatenate(xs, axis=1), 1, 0)
            block = lax.rsqrt(dist.astype(bf16))
            term = dot(block, jnp.concatenate(ds, axis=1), 1, 1)
            acc = term if acc is None else acc + term
        return acc.T

    def far_leaf(i):
        node1 = i // 4
        g0 = dot(grade[node1], t1[node1, i % 4], 1, 0).astype(bf16)
        return dot(g0, basis[i], 1, 0)

    def inner(g, carry):
        for u in range(UNROLL):
            j = g * UNROLL + u
            nearf[j] = near_leaf(j + REACH)
        return carry

    count = leaves - 2 * REACH
    lax.fori_loop(0, count // UNROLL, inner, 0)

    for c in halos + more:
        c.wait()
    for c in loads[6:]:
        c.wait()
    for j in range(REACH):
        cols = slice(j * 128, (j + 1) * 128)
        prepare(j, dleft[:, cols], gleft[0:4, cols], False)
        prepare(REACH + leaves + j, dright[:, cols], gright[0:4, cols], False)

    spans = ((0, n1), (n1, n2), (n1 + n2, 1))
    bases = (0, 3 * n1, 3 * (n1 + n2))
    for (lo, n), base in zip(spans, bases):
        for m in range(n):
            wide[base + m] = cleft[lo + m]
            wide[base + n + m] = own[lo + m]
            wide[base + 2 * n + m] = cright[lo + m]

    def couple(c, p, level, n):
        cells = spans[level][1]
        acc = None
        for k in range(4):
            o = wrap(p(n, k) - (me * cells + n), cells * shards)
            place = jnp.clip(cells + n + o, 0, 3 * cells - 1)
            term = dot(wide[bases[level] + place], c[n, k], 1, 1)
            acc = term if acc is None else acc + term
        return acc

    node = me // 4
    field4 = None
    for k in range(4):
        q4 = p4[node, k]
        acc = None
        for q in range(4):
            d = wrap(4 * q4 + q - me, shards)
            slot = jnp.where(d < 0, d + shards, d) if shards <= 2 * FAR + 1 else jnp.clip(d + FAR, 0, 2 * FAR)
            term = dot(three[slot], t4[q4, q], 1, 1)
            acc = term if acc is None else acc + term
        term = dot(acc.astype(bf16), c4[node, k], 1, 1)
        field4 = term if field4 is None else field4 + term
    g4 = field4.astype(bf16)
    f3 = couple(c3, lambda n, k: p3[n, k], 2, 0)
    f2 = [couple(c2, lambda n, k: p2[n, k], 1, m) for m in range(n2)]
    f1 = [couple(c1, lambda n, k: p1[k, n], 0, n) for n in range(n1)]
    g3 = (f3 + dot(g4, t4[node, me % 4], 1, 0)).astype(bf16)
    g2 = [(f2[m] + dot(g3, t3[0, m], 1, 0)).astype(bf16) for m in range(n2)]
    for n in range(n1):
        grade[n] = (f1[n] + dot(g2[n // 4], t2[n // 4, n % 4], 1, 0)).astype(bf16)

    def store(i, value):
        out[:, pl.ds(pl.multiple_of(i * 128, 128), 128)] = value.astype(bf16)

    def outer(g, carry):
        for u in range(UNROLL):
            j = g * UNROLL + u
            i = jnp.where(j < REACH, j, j + count)
            store(i, near_leaf(i) + far_leaf(i))
        return carry

    lax.fori_loop(0, 2 * REACH // UNROLL, outer, 0)

    def finish(g, carry):
        for u in range(16):
            j = g * 16 + u
            store(j + REACH, nearf[j] + far_leaf(j + REACH))
        return carry

    lax.fori_loop(0, count // 16, finish, 0)


VM = pl.BlockSpec(memory_space=pltpu.VMEM)
HB = pl.BlockSpec(memory_space=pltpu.HBM)
SM = pl.BlockSpec(memory_space=pltpu.SMEM)


def body(
    densities, geometry, near_index, leaf_basis,
    transfer_one, coupling_one, partners_one,
    transfer_two, coupling_two, partners_two,
    transfer_three, coupling_three, partners_three,
    transfer_four, coupling_four, partners_four,
):
    shards = lax.axis_size(AXES)
    leaves, rank, _ = leaf_basis.shape
    rhs, points = densities.shape
    n1, n2 = transfer_one.shape[0], transfer_two.shape[0]
    nodes = n1 + n2 + 1
    width = REACH * 128
    offsets, slots = peers(shards)
    wide = leaves + 2 * REACH
    arrays = (
        densities, geometry, leaf_basis, transfer_one, transfer_two, transfer_three, transfer_four,
        coupling_one, coupling_two, coupling_three, coupling_four,
    )
    coef = pltpu.VMEM((nodes, rhs, rank), bf16)
    return pl.pallas_call(
        functools.partial(whole_kernel, shards, lax.axis_size("rhs"), lax.axis_size("sub")),
        out_shape=jax.ShapeDtypeStruct((rhs, points), bf16),
        in_specs=[SM] * 5 + [HB] * len(arrays),
        out_specs=VM,
        scratch_shapes=[pltpu.VMEM(v.shape, v.dtype) for v in arrays] + [
            coef, coef, coef,
            pltpu.VMEM((slots, rhs, rank), bf16),
            pltpu.VMEM((rhs, width), bf16),
            pltpu.VMEM((rhs, width), bf16),
            pltpu.VMEM((16, width), bf16),
            pltpu.VMEM((16, width), bf16),
            pltpu.VMEM((leaves, rhs, rank), bf16),
            pltpu.VMEM((2, 16, width), bf16),
            pltpu.VMEM((3 * nodes, rhs, rank), bf16),
            pltpu.VMEM((wide, rhs, 128), bf16),
            pltpu.VMEM((wide, 8, 128), f32),
            pltpu.VMEM((wide, 8, 128), f32),
            pltpu.VMEM((leaves, 128, 16), bf16),
            pltpu.VMEM((n1, rhs, rank), bf16),
            pltpu.VMEM((leaves - 2 * REACH, rhs, 128), f32),
            pltpu.SemaphoreType.DMA((len(arrays),)),
            pltpu.SemaphoreType.DMA((6 + len(offsets),)),
            pltpu.SemaphoreType.DMA((6 + len(offsets),)),
        ],
        compiler_params=pltpu.CompilerParams(
            vmem_limit_bytes=48 * 2**20, collective_id=0, has_side_effects=True
        ),
        name="whole",
    )(near_index.T, partners_one.T, partners_two, partners_three, partners_four, *arrays)


def solution(mesh):
    every = ("groups", "leaf", "rhs", "sub")
    split = lambda n: P(every, *([None] * n))
    level = [split(3), split(3), split(1)]
    in_specs = (
        P(None, every), P(None, every), split(1), split(2),
        *level, *level, *level,
        P("groups", None, None, None), P("groups", None, None, None), P("groups", None),
    )
    return jax.shard_map(body, mesh=mesh, in_specs=in_specs, out_specs=P(None, every), check_vma=False)
```

```python
import functools

import jax
import jax.numpy as jnp
from jax import lax
from jax.experimental import pallas as pl
from jax.experimental.pallas import tpu as pltpu
from jax.sharding import PartitionSpec as P

AXES = ("leaf", "rhs", "sub")
REACH = 16
FAR = 11
SPACING2 = 0.01
SMOOTH = 0.0025
GROUP = 2
UNROLL = 8
f32 = jnp.float32
bf16 = jnp.bfloat16


def dot(a, b, ca, cb):
    return lax.dot_general(a, b, (((ca,), (cb,)), ((), ())), preferred_element_type=f32)


def wrap(d, total):
    d = jnp.where(d >= total // 2, d - total, d)
    return jnp.where(d < -(total // 2), d + total, d)


def split3(v):
    hi = v.astype(bf16).astype(f32)
    r1 = v - hi
    mid = r1.astype(bf16).astype(f32)
    return r1, r1 - mid


def peers(shards):
    if shards <= 2 * FAR + 1:
        return list(range(1, shards)), shards
    return [d for d in range(-FAR, FAR + 1) if d], 2 * FAR + 1


def slot_of(d, shards):
    if shards <= 2 * FAR + 1:
        return d % shards
    return d + FAR


def whole_kernel(
    shards, rhs_axis, sub_axis,
    near_index, p1, p2, p3, p4,
    dens_hbm, geom_hbm, basis_hbm, t1_hbm, t2_hbm, t3_hbm, t4_hbm, c1_hbm, c2_hbm, c3_hbm, c4_hbm,
    out,
    dens, geom, basis, t1, t2, t3, t4, c1, c2, c3, c4,
    own, cleft, cright, three, dleft, dright, gleft, gright,
    c0, stage, wide, densw, fa, fb, tf, grade, nearf,
    load, send, recv,
):
    leaves = basis.shape[0]
    near = near_index.shape[0]
    total = leaves * shards
    n1, n2 = t1.shape[0], t2.shape[0]
    nodes = own.shape[0]
    width = dleft.shape[1]
    points = dens.shape[1]
    me = lax.axis_index(AXES)
    offsets, _ = peers(shards)

    pairs = (
        (dens_hbm, dens), (geom_hbm, geom), (basis_hbm, basis), (t1_hbm, t1), (t2_hbm, t2), (t3_hbm, t3),
        (t4_hbm, t4), (c1_hbm, c1), (c2_hbm, c2), (c3_hbm, c3), (c4_hbm, c4),
    )
    loads = [pltpu.make_async_copy(src, dst, load.at[x]) for x, (src, dst) in enumerate(pairs)]
    for c in loads:
        c.start()

    def at(step):
        s = lax.rem(me + step + shards, shards)
        return {
            "leaf": s // (rhs_axis * sub_axis),
            "rhs": (s // sub_axis) % rhs_axis,
            "sub": s % sub_axis,
        }

    def copy(src, dst, index, step):
        return pltpu.make_async_remote_copy(
            src_ref=src, dst_ref=dst, send_sem=send.at[index], recv_sem=recv.at[index],
            device_id=at(step), device_id_type=pl.DeviceIdType.MESH,
        )

    barrier = pltpu.get_barrier_semaphore()
    for d in offsets:
        pl.semaphore_signal(barrier, inc=1, device_id=at(d), device_id_type=pl.DeviceIdType.MESH)
    stage[...] = jnp.zeros_like(stage)
    loads[0].wait()
    loads[1].wait()
    stage[0, 0:4] = geom[:, points - width :]
    stage[1, 0:4] = geom[:, :width]
    loads[2].wait()

    def leaf_coefs(g, carry):
        for u in range(16):
            i = g * 16 + u
            cols = pl.ds(pl.multiple_of(i * 128, 128), 128)
            c0[i] = dot(dens[:, cols], basis[i], 1, 1).astype(bf16)
        return carry

    lax.fori_loop(0, leaves // 16, leaf_coefs, 0)
    for c in loads[3:6]:
        c.wait()

    def lift(t, n, source, base, into):
        acc = None
        for q in range(4):
            term = dot(source[base + 4 * n + q], t[n, q], 1, 1)
            acc = term if acc is None else acc + term
        own[into + n] = acc.astype(bf16)

    for n in range(n1):
        lift(t1, n, c0, 0, 0)
    for n in range(n2):
        lift(t2, n, own, 0, n1)
    lift(t3, 0, own, n1, n1 + n2)
    pl.semaphore_wait(barrier, len(offsets))

    halos = [
        copy(dens.at[:, pl.ds(points - width, width)], dleft, 0, 1),
        copy(dens.at[:, pl.ds(0, width)], dright, 1, -1),
        copy(stage.at[0], gleft, 2, 1),
        copy(stage.at[1], gright, 3, -1),
    ]
    more = [copy(own.at[nodes - 1], three.at[slot_of(-d, shards)], 6 + x, d) for x, d in enumerate(offsets)]
    more += [copy(own, cleft, 4, 1), copy(own, cright, 5, -1)]
    for c in halos + more:
        c.start()
    three[slot_of(0, shards)] = own[nodes - 1]

    row8 = lax.broadcasted_iota(jnp.int32, (8, 128), 0)
    first = (row8 == 0) | (row8 == 3) | (row8 >= 6)
    second = (row8 == 1) | (row8 == 4)

    def prepare(slot, d, gb, mine):
        densw[slot] = d * gb[3:4]
        g = gb.astype(f32)
        a8, y8, z8 = (jnp.broadcast_to(g[r : r + 1], (8, 128)) for r in range(3))
        square = SPACING2 * a8 * a8 + y8 * y8 + z8 * z8
        fa[slot] = jnp.where(
            row8 < 3, square + SMOOTH,
            jnp.where(row8 < 6, (-2.0 * SPACING2) * a8, jnp.where(row8 == 6, -2.0 * y8, -2.0 * z8)),
        )
        fb[slot] = jnp.where(row8 < 3, (2.0 * SPACING2) * a8, jnp.where(row8 < 6, -2.0 * SPACING2, 0.0))
        if mine:
            r1, r2 = split3(square)
            upper = jnp.where(row8 < 3, 1.0, jnp.where(row8 < 6, a8, jnp.where(row8 == 6, y8, z8)))
            lower = jnp.where(row8 == 0, square, jnp.where(row8 == 1, r1, jnp.where(row8 == 2, r2, 0.0)))
            tf[slot - REACH] = jnp.concatenate([upper, lower], axis=0).T.astype(bf16)

    def prepare_own(g, carry):
        for u in range(16):
            j = g * 16 + u
            cols = pl.ds(pl.multiple_of(j * 128, 128), 128)
            prepare(REACH + j, dens[:, cols], geom[:, cols], True)
        return carry

    lax.fori_loop(0, leaves // 16, prepare_own, 0)

    quad = jnp.where(row8 < 3, SPACING2, 0.0)
    tail = jnp.where(row8 < 3, 1.0, 0.0)

    def source(i, k):
        o = wrap(near_index[k, i] - (me * leaves + i), total)
        pos = jnp.clip(i + REACH + o, 0, leaves + 2 * REACH - 1)
        of = o.astype(f32)
        v = fa[pos] + of * (fb[pos] + of * quad)
        r1, r2 = split3(v)
        x = jnp.where(first, v, jnp.where(second, r1, r2))
        return jnp.concatenate([x, tail], axis=0).astype(bf16), densw[pos]

    def near_leaf(i):
        target = tf[i]
        acc = None
        for k in range(0, near, GROUP):
            xs, ds = zip(*[source(i, k + u) for u in range(GROUP)])
            dist = dot(target, jnp.concatenate(xs, axis=1), 1, 0)
            block = lax.rsqrt(dist.astype(bf16))
            term = dot(block, jnp.concatenate(ds, axis=1), 1, 1)
            acc = term if acc is None else acc + term
        return acc.T

    def far_leaf(i):
        node1 = i // 4
        g0 = dot(grade[node1], t1[node1, i % 4], 1, 0).astype(bf16)
        return dot(g0, basis[i], 1, 0)

    def inner(g, carry):
        for u in range(UNROLL):
            j = g * UNROLL + u
            nearf[j] = near_leaf(j + REACH)
        return carry

    count = leaves - 2 * REACH
    lax.fori_loop(0, count // UNROLL, inner, 0)

    for c in halos + more:
        c.wait()
    for c in loads[6:]:
        c.wait()
    for j in range(REACH):
        cols = slice(j * 128, (j + 1) * 128)
        prepare(j, dleft[:, cols], gleft[0:4, cols], False)
        prepare(REACH + leaves + j, dright[:, cols], gright[0:4, cols], False)

    spans = ((0, n1), (n1, n2), (n1 + n2, 1))
    bases = (0, 3 * n1, 3 * (n1 + n2))
    for (lo, n), base in zip(spans, bases):
        for m in range(n):
            wide[base + m] = cleft[lo + m]
            wide[base + n + m] = own[lo + m]
            wide[base + 2 * n + m] = cright[lo + m]

    def couple(c, p, level, n):
        cells = spans[level][1]
        acc = None
        for k in range(4):
            o = wrap(p(n, k) - (me * cells + n), cells * shards)
            place = jnp.clip(cells + n + o, 0, 3 * cells - 1)
            term = dot(wide[bases[level] + place], c[n, k], 1, 1)
            acc = term if acc is None else acc + term
        return acc

    node = me // 4
    field4 = None
    for k in range(4):
        q4 = p4[node, k]
        acc = None
        for q in range(4):
            d = wrap(4 * q4 + q - me, shards)
            slot = jnp.where(d < 0, d + shards, d) if shards <= 2 * FAR + 1 else jnp.clip(d + FAR, 0, 2 * FAR)
            term = dot(three[slot], t4[q4, q], 1, 1)
            acc = term if acc is None else acc + term
        term = dot(acc.astype(bf16), c4[node, k], 1, 1)
        field4 = term if field4 is None else field4 + term
    g4 = field4.astype(bf16)
    f3 = couple(c3, lambda n, k: p3[n, k], 2, 0)
    f2 = [couple(c2, lambda n, k: p2[n, k], 1, m) for m in range(n2)]
    f1 = [couple(c1, lambda n, k: p1[k, n], 0, n) for n in range(n1)]
    g3 = (f3 + dot(g4, t4[node, me % 4], 1, 0)).astype(bf16)
    g2 = [(f2[m] + dot(g3, t3[0, m], 1, 0)).astype(bf16) for m in range(n2)]
    for n in range(n1):
        grade[n] = (f1[n] + dot(g2[n // 4], t2[n // 4, n % 4], 1, 0)).astype(bf16)

    def store(i, value):
        out[:, pl.ds(pl.multiple_of(i * 128, 128), 128)] = value.astype(bf16)

    def outer(g, carry):
        for u in range(UNROLL):
            j = g * UNROLL + u
            i = jnp.where(j < REACH, j, j + count)
            store(i, near_leaf(i) + far_leaf(i))
        return carry

    lax.fori_loop(0, 2 * REACH // UNROLL, outer, 0)

    def finish(g, carry):
        for u in range(16):
            j = g * 16 + u
            store(j + REACH, nearf[j] + far_leaf(j + REACH))
        return carry

    lax.fori_loop(0, count // 16, finish, 0)


VM = pl.BlockSpec(memory_space=pltpu.VMEM)
HB = pl.BlockSpec(memory_space=pltpu.HBM)
SM = pl.BlockSpec(memory_space=pltpu.SMEM)


def body(
    densities, geometry, near_index, leaf_basis,
    transfer_one, coupling_one, partners_one,
    transfer_two, coupling_two, partners_two,
    transfer_three, coupling_three, partners_three,
    transfer_four, coupling_four, partners_four,
):
    shards = lax.axis_size(AXES)
    leaves, rank, _ = leaf_basis.shape
    rhs, points = densities.shape
    n1, n2 = transfer_one.shape[0], transfer_two.shape[0]
    nodes = n1 + n2 + 1
    width = REACH * 128
    offsets, slots = peers(shards)
    wide = leaves + 2 * REACH
    arrays = (
        densities, geometry, leaf_basis, transfer_one, transfer_two, transfer_three, transfer_four,
        coupling_one, coupling_two, coupling_three, coupling_four,
    )
    coef = pltpu.VMEM((nodes, rhs, rank), bf16)
    return pl.pallas_call(
        functools.partial(whole_kernel, shards, lax.axis_size("rhs"), lax.axis_size("sub")),
        out_shape=jax.ShapeDtypeStruct((rhs, points), bf16),
        in_specs=[SM] * 5 + [HB] * len(arrays),
        out_specs=VM,
        scratch_shapes=[pltpu.VMEM(v.shape, v.dtype) for v in arrays] + [
            coef, coef, coef,
            pltpu.VMEM((slots, rhs, rank), bf16),
            pltpu.VMEM((rhs, width), bf16),
            pltpu.VMEM((rhs, width), bf16),
            pltpu.VMEM((16, width), bf16),
            pltpu.VMEM((16, width), bf16),
            pltpu.VMEM((leaves, rhs, rank), bf16),
            pltpu.VMEM((2, 16, width), bf16),
            pltpu.VMEM((3 * nodes, rhs, rank), bf16),
            pltpu.VMEM((wide, rhs, 128), bf16),
            pltpu.VMEM((wide, 8, 128), f32),
            pltpu.VMEM((wide, 8, 128), f32),
            pltpu.VMEM((leaves, 128, 16), bf16),
            pltpu.VMEM((n1, rhs, rank), bf16),
            pltpu.VMEM((leaves - 2 * REACH, rhs, 128), f32),
            pltpu.SemaphoreType.DMA((len(arrays),)),
            pltpu.SemaphoreType.DMA((6 + len(offsets),)),
            pltpu.SemaphoreType.DMA((6 + len(offsets),)),
        ],
        compiler_params=pltpu.CompilerParams(
            vmem_limit_bytes=63 * 2**20, collective_id=0, has_side_effects=True
        ),
        name="whole",
    )(near_index.T, partners_one.T, partners_two, partners_three, partners_four, *arrays)


def solution(mesh):
    every = ("groups", "leaf", "rhs", "sub")
    split = lambda n: P(every, *([None] * n))
    level = [split(3), split(3), split(1)]
    in_specs = (
        P(None, every), P(None, every), split(1), split(2),
        *level, *level, *level,
        P("groups", None, None, None), P("groups", None, None, None), P("groups", None),
    )
    return jax.shard_map(body, mesh=mesh, in_specs=in_specs, out_specs=P(None, every), check_vma=False)
```
